32 devices in a mesh: pipe: 8 (over z, x), tensor: 4 (over y, core).
Axes of the slice: x: 2, y: 2, z: 4, core: 2. Of those that a mesh axis runs over, the one named last changes fastest.
Arguments:
- section_weights: bfloat16 [8, 2, 4096, 4096], P('pipe', None, 'tensor'), may hold values from -0.09375 to 0.09375
- context: bfloat16 [8, 2, 768, 4096], P('pipe', None, None, 'tensor'), may hold values from -3 to 3
- grad_out: bfloat16 [8, 2, 768, 4096], P('pipe', None, 'tensor'), may hold values from -3 to 3
Outputs:
- weight_grad: bfloat16 [8, 4096, 4096], P('pipe', 'tensor')
- input_grad: bfloat16 [8, 2, 768, 4096], P('pipe', None, None, 'tensor')
The draws below stay inside these ranges and needn't reach their ends.
All inputs are finite; a program needn't handle non-finite values.
Results may differ from the reference program's by a relative error of at most 0.001.
Values may be sent and summed in bfloat16 or wider, within the bound.
A program may use at most 192 MiB of HBM per device.

```python
import jax
import jax.numpy as jnp
from jax import lax

DI = 4096
DO = 4096
TOK = 768
SECTIONS = 8


def level_of(stream_key, shape, cuts, low, largest):
    def one(dim, shards_of):
        draws = jax.random.uniform(jax.random.fold_in(jax.random.fold_in(stream_key, 6), dim), (shards_of,), jnp.float32, low / len(cuts), largest / len(cuts))
        return jnp.repeat(jnp.exp(draws), shape[dim] // shards_of).reshape((-1,) + (1,) * (len(shape) - dim - 1))

    factor_of = one(*cuts[0])
    for cut in cuts[1:]:
        factor_of = factor_of * one(*cut)
    return factor_of


def noise(stream_key, dims, scale, limit, shards=(), kind=jnp.bfloat16):
    loudness = level_of(stream_key, dims, shards, -0.22, 0.18) if shards else 1.0
    entries = jax.random.normal(stream_key, dims, jnp.float32) * scale * loudness
    return jnp.minimum(jnp.maximum(entries, -limit), limit).astype(kind)


def setup_inputs(seed: int = 0) -> dict:
    streams_of = jax.random.split(jax.random.key(seed), 4)
    return {
        "section_weights": noise(streams_of[0], (SECTIONS, 2, DI, DO), DO ** -0.5, 0.09375, ((0, 8), (2, 4))),
        "context": noise(streams_of[1], (SECTIONS, 2, TOK, DI), 0.2, 3.0, ((0, 8), (3, 4))),
        "grad_out": noise(streams_of[2], (SECTIONS, 2, TOK, DO), 0.2, 3.0, ((0, 8), (2, 4))),
    }


def reference(section_weights, context, grad_out):
    sections = context.shape[0]

    def section_grad(position):
        mirror = sections - 1 - position
        down = jnp.dot(context[position, 0].T, grad_out[position, 0], preferred_element_type=jnp.float32)
        up = jnp.dot(context[mirror, 1].T, grad_out[mirror, 1], preferred_element_type=jnp.float32)
        return (down + up).astype(jnp.bfloat16)
    weight_grad = lax.map(section_grad, jnp.arange(sections, dtype=jnp.int32))

    def backward(position):
        first = jnp.dot(grad_out[position, 0], section_weights[position, 0].T, preferred_element_type=jnp.float32)
        second = jnp.dot(grad_out[position, 1], section_weights[position, 1].T, preferred_element_type=jnp.float32)
        return jnp.stack([first, second]).astype(jnp.bfloat16)
    local = lax.map(backward, jnp.arange(sections, dtype=jnp.int32))
    empty = jnp.zeros_like(local[:1, 0])
    down_recv = jnp.concatenate([local[1:, 0], empty], axis=0)
    up_recv = jnp.concatenate([empty, local[:-1, 1]], axis=0)
    input_grad = jnp.stack([down_recv, up_recv], axis=1)
    return (weight_grad, input_grad)
```

```python
import jax
import jax.numpy as jnp
from jax import lax
from jax.sharding import PartitionSpec as P


def from_behind(value, axis, by):
    count = lax.axis_size(axis)
    pairs = [(i, i + by) for i in range(count) if 0 <= i + by < count]
    return lax.ppermute(value, axis, pairs)


def from_mirror(value, axis):
    count = lax.axis_size(axis)
    return lax.ppermute(value, axis, [(i, count - 1 - i) for i in range(count)])


def weight_part(rows, gradient):
    return jnp.einsum("td,to->do", rows, gradient, preferred_element_type=jnp.float32)


def back_part(gradient, weights):
    return jnp.einsum(
        "to,do->td", gradient, weights, preferred_element_type=jnp.float32
    ).astype(jnp.bfloat16)


def shards(section_weights, context, grad_out):
    far_grad = from_mirror(grad_out[0, 1], "pipe")
    far_context = from_mirror(context[0, 1], "pipe")
    up = lax.all_gather(grad_out[0, 1], "tensor", axis=0, tiled=True)
    down = lax.all_gather(grad_out[0, 0], "tensor", axis=0, tiled=True)
    from_prior = from_behind(back_part(up, section_weights[0, 1]), "pipe", 1)
    from_next = from_behind(back_part(down, section_weights[0, 0]), "pipe", -1)
    far = lax.all_gather(far_grad, "tensor", axis=0, tiled=True)
    total = weight_part(context[0, 0], down) + weight_part(far_context, far)
    weight_grad = total.astype(jnp.bfloat16)[None]
    input_grad = jnp.stack([from_next, from_prior])[None]
    return (weight_grad, input_grad)


def solution(mesh):
    placed = (
        P("pipe", None, "tensor", None),
        P("pipe", None, None, "tensor"),
        P("pipe", None, "tensor", None),
    )
    return jax.shard_map(
        shards,
        mesh=mesh,
        in_specs=placed,
        out_specs=(P("pipe", "tensor", None), P("pipe", None, None, "tensor")),
        check_vma=False,
    )
```

```python
import functools

import jax
import jax.numpy as jnp
from jax import lax
from jax.experimental import pallas as pl
from jax.experimental.pallas import tpu as pltpu
from jax.sharding import PartitionSpec as P

MESH = pl.DeviceIdType.MESH
UP, DOWN, FAR = 1, 0, 2


def flip(index, bit):
    return index + bit - 2 * bit * ((index // bit) % 2)


def kernel(
    pipes, group, w_ref, c_ref, g_ref, wg_ref, ig_ref,
    grads, weights, context, far_context, back, turned, total,
    gather_send, gather_recv, far_send, far_recv, column_send, column_recv,
    relay_send, relay_recv, own_sem, load_sem, zero_sem, store_sem,
):
    p = lax.axis_index("pipe")
    t = lax.axis_index("tensor")
    mirror = pipes - 1 - p
    share = g_ref.shape[2]
    tokens, width_out = grads.shape[1:]
    width_in = weights.shape[0]
    block = turned.shape[0]
    blocks = width_in // block
    bits = []
    while (group >> (len(bits) + 1)) > 0:
        bits.append(group >> (len(bits) + 1))
    has_prior, has_next = p > 0, p < pipes - 1

    def piece_rows(piece):
        return pl.ds(pl.multiple_of(piece * share, 16), share)

    def gather_copies(stream, level):
        partner = flip(t, bits[level])
        copies = []
        for m in range(1 << level):
            piece = t
            for j in range(level):
                if (m >> j) & 1:
                    piece = flip(piece, bits[j])
            k = (1 << level) - 1 + m
            rows = piece_rows(piece)
            source = grads.at[stream, rows]
            if m == 0 and stream != FAR:
                source = g_ref.at[0, stream]
            copies.append(
                pltpu.make_async_remote_copy(
                    src_ref=source,
                    dst_ref=grads.at[stream, rows],
                    send_sem=gather_send.at[stream, k],
                    recv_sem=gather_recv.at[stream, k],
                    device_id=(p, partner),
                    device_id_type=MESH,
                )
            )
        return copies

    def gather_wait(stream, level):
        partner = flip(t, bits[level])
        for m in range(1 << level):
            piece = partner
            for j in range(level):
                if (m >> j) & 1:
                    piece = flip(piece, bits[j])
            k = (1 << level) - 1 + m
            rows = piece_rows(piece)
            pltpu.make_async_remote_copy(
                src_ref=grads.at[stream, rows],
                dst_ref=grads.at[stream, rows],
                send_sem=gather_send.at[stream, k],
                recv_sem=gather_recv.at[stream, k],
                device_id=(p, partner),
                device_id_type=MESH,
            ).wait_recv()

    far_copy = pltpu.make_async_remote_copy(
        src_ref=g_ref.at[0, UP],
        dst_ref=grads.at[FAR, piece_rows(t)],
        send_sem=far_send.at[0],
        recv_sem=far_recv.at[0],
        device_id=(mirror, t),
        device_id_type=MESH,
    )

    def column_copy(c):
        columns = pl.ds(c * block, block)
        return pltpu.make_async_remote_copy(
            src_ref=c_ref.at[0, UP, :, columns],
            dst_ref=far_context.at[:, columns],
            send_sem=column_send.at[c],
            recv_sem=column_recv.at[c],
            device_id=(mirror, t),
            device_id_type=MESH,
        )

    def relay(replica, to):
        return pltpu.make_async_remote_copy(
            src_ref=back.at[replica],
            dst_ref=ig_ref.at[0, replica],
            send_sem=relay_send.at[replica],
            recv_sem=relay_recv.at[replica],
            device_id=(to, t),
            device_id_type=MESH,
        )

    def load_weights(replica):
        return pltpu.make_async_copy(w_ref.at[0, replica], weights, load_sem.at[0])

    def zero(replica):
        return pltpu.make_async_copy(back.at[replica], ig_ref.at[0, 1 - replica], zero_sem.at[0])

    def multiply_back(replica):
        half = tokens // 2

        @pl.loop(0, blocks)
        def _(c):
            columns = pl.ds(pl.multiple_of(c * block, block), block)

            @pl.loop(0, 2)
            def _(h):
                rows = pl.ds(pl.multiple_of(h * half, half), half)
                product = lax.dot_general(
                    grads[replica, rows, :], weights[columns, :],
                    (((1,), (1,)), ((), ())), preferred_element_type=jnp.float32,
                )
                back[replica, rows, columns] = product.astype(back.dtype)

    slab = 512
    slabs = width_out // slab

    own = [
        pltpu.make_async_copy(g_ref.at[0, r], grads.at[r, piece_rows(t)], own_sem.at[r])
        for r in (0, 1)
    ]
    load_context = pltpu.make_async_copy(c_ref.at[0, DOWN], context, load_sem.at[1])

    barrier = pltpu.get_barrier_semaphore()
    pl.semaphore_signal(barrier, inc=1, device_id=(mirror, t), device_id_type=MESH)
    for bit in bits:
        pl.semaphore_signal(barrier, inc=1, device_id=(p, flip(t, bit)), device_id_type=MESH)

    for beside in (lax.rem(p + 1, pipes), lax.rem(p + pipes - 1, pipes)):
        pl.semaphore_signal(barrier, inc=1, device_id=(beside, t), device_id_type=MESH)

    own[UP].start()
    own[DOWN].start()
    load_weights(UP).start()
    load_context.start()
    pl.semaphore_wait(barrier, 3 + len(bits))

    far_copy.start()
    gathers = {(s, l): gather_copies(s, l) for s in range(3) for l in range(len(bits))}
    gathers[UP, 0][0].start()
    for level in range(1, len(bits)):
        gathers[UP, level][0].start()
        gathers[DOWN, level][0].start()

    def finish_gather(stream):
        for level in range(len(bits)):
            gather_wait(stream, level)
            if level + 1 < len(bits):
                for later in range(level + 1, len(bits)):
                    for m in range(1 << level, 1 << (level + 1)):
                        gathers[stream, later][m].start()

    gathers[UP, 0][0].wait_send()
    gathers[DOWN, 0][0].start()
    finish_gather(UP)
    own[UP].wait()
    load_weights(UP).wait()
    multiply_back(UP)
    load_weights(DOWN).start()
    far_copy.wait_send()
    for c in range(blocks):
        column_copy(c).start()

    @pl.when(has_next)
    def _():
        relay(UP, p + 1).start()

    @pl.when(p == pipes - 1)
    def _():
        back[UP] = jnp.zeros(back.shape[1:], back.dtype)
        zero(UP).start()

    finish_gather(DOWN)
    own[DOWN].wait()
    far_copy.wait_recv()
    for level in range(len(bits)):
        gathers[FAR, level][0].start()

    load_weights(DOWN).wait()
    multiply_back(DOWN)

    @pl.when(has_prior)
    def _():
        relay(DOWN, p - 1).start()

    @pl.when(p == 0)
    def _():
        back[DOWN] = jnp.zeros(back.shape[1:], back.dtype)
        zero(DOWN).start()

    load_context.wait()

    @pl.loop(0, blocks)
    def _(c):
        columns = pl.ds(pl.multiple_of(c * block, block), block)
        turned[...] = context[:, columns].T

        @pl.loop(0, slabs)
        def _(n):
            part = pl.ds(pl.multiple_of(n * slab, slab), slab)
            total[columns, part] = jnp.dot(
                turned[...], grads[DOWN, :, part], preferred_element_type=jnp.float32
            )

    finish_gather(FAR)
    stores = []
    for c in range(blocks):
        column_copy(c).wait_recv()
        columns = pl.ds(c * block, block)
        turned[...] = far_context[:, columns].T

        @pl.loop(0, slabs)
        def _(n):
            part = pl.ds(pl.multiple_of(n * slab, slab), slab)
            weights[columns, part] = (
                total[columns, part]
                + jnp.dot(turned[...], grads[FAR, :, part], preferred_element_type=jnp.float32)
            ).astype(weights.dtype)

        store = pltpu.make_async_copy(
            weights.at[columns], wg_ref.at[0, columns], store_sem.at[c]
        )
        store.start()
        stores.append(store)

    for store in stores:
        store.wait()
    far_copy_done = [gathers[UP, l][m] for l in range(1, len(bits)) for m in range(1 << l)]
    far_copy_done += [gathers[s, l][m] for s in (DOWN, FAR) for l in range(len(bits)) for m in range(1 << l)]
    far_copy_done += [column_copy(c) for c in range(blocks)]
    for copy in far_copy_done:
        copy.wait_send()

    @pl.when(has_next)
    def _():
        relay(UP, p + 1).wait_send()
        relay(DOWN, p + 1).wait_recv()

    @pl.when(has_prior)
    def _():
        relay(DOWN, p - 1).wait_send()
        relay(UP, p - 1).wait_recv()

    @pl.when(p == pipes - 1)
    def _():
        zero(UP).wait()

    @pl.when(p == 0)
    def _():
        zero(DOWN).wait()


def shards(pipes, group, section_weights, context, grad_out):
    width_in, width_out = section_weights.shape[2:]
    tokens = context.shape[2]
    block = min(256, width_in)
    blocks = width_in // block
    kind = jnp.bfloat16
    dma = pltpu.SemaphoreType.DMA
    anywhere = pl.BlockSpec(memory_space=pl.ANY)
    return pl.pallas_call(
        functools.partial(kernel, pipes, group),
        out_shape=(
            jax.ShapeDtypeStruct((1, width_in, width_out), kind),
            jax.ShapeDtypeStruct((1, 2, tokens, width_in), kind),
        ),
        in_specs=[anywhere] * 3,
        out_specs=(anywhere, anywhere),
        scratch_shapes=[
            pltpu.VMEM((3, tokens, width_out), kind),
            pltpu.VMEM((width_in, width_out), kind),
            pltpu.VMEM((tokens, width_in), kind),
            pltpu.VMEM((tokens, width_in), kind),
            pltpu.VMEM((2, tokens, width_in), kind),
            pltpu.VMEM((block, tokens), kind),
            pltpu.VMEM((width_in, width_out), jnp.float32),
            dma((3, group - 1)),
            dma((3, group - 1)),
            dma((1,)),
            dma((1,)),
            dma((blocks,)),
            dma((blocks,)),
            dma((2,)),
            dma((2,)),
            dma((2,)),
            dma((2,)),
            dma((1,)),
            dma((blocks,)),
        ],
        compiler_params=pltpu.CompilerParams(
            collective_id=0, has_side_effects=True, vmem_limit_bytes=58 * 2**20
        ),
        cost_estimate=pl.CostEstimate(
            flops=8 * tokens * width_in * width_out,
            bytes_accessed=2 * (3 * width_in * width_out + 9 * tokens * width_in),
            transcendentals=0,
        ),
    )(section_weights, context, grad_out)


def solution(mesh):
    placed = (
        P("pipe", None, "tensor", None),
        P("pipe", None, None, "tensor"),
        P("pipe", None, "tensor", None),
    )
    return jax.shard_map(
        functools.partial(shards, mesh.shape["pipe"], mesh.shape["tensor"]),
        mesh=mesh,
        in_specs=placed,
        out_specs=(P("pipe", "tensor", None), P("pipe", None, None, "tensor")),
        check_vma=False,
    )
```
